32 devices in a mesh: groups: 2 (over y), rows: 8 (over z, x), cols: 1, sub: 2 (over core).
Axes of the slice: x: 2, y: 2, z: 4, core: 2. Of those that a mesh axis runs over, the one named last changes fastest.
Arguments:
- points: float32 [256, 65536], P('cols', ('groups', 'rows', 'sub')), parts along dimension 1, may hold values from -17 to 17
- start_block: float32 [256, 64], P('cols'), may hold values from -6 to 6
- median_order: int32 [32, 2048], P(('groups', 'rows', 'sub')), parts along dimension 0, may hold values from 0 to 2047, each once within a row
Outputs:
- moved_points: float32 [256, 65536], P('cols', ('groups', 'rows', 'sub')), parts along dimension 1
- moved_coords: float32 [64, 65536], P(None, ('groups', 'rows', 'sub')), parts along dimension 1
The draws below stay inside these ranges and needn't reach their ends.
There are 2 independent parts, one for each index of `groups`. The reference program is written for one: setup_inputs(seed, part) draws one part's arguments, and reference() takes and returns one part's arrays. A program takes and returns all parts, laid end to end along the dimension named above; an argument that names none is the same for every part. Nothing has to cross between parts.
Inputs may be any that keep to these rules, and one draw needn't show every extreme that they name: `median_order`: each row is a permutation of the local positions.
All inputs are finite; a program needn't handle non-finite values.
Results may differ from the reference program's by a relative error of at most 0.00016.
Values sent between devices are 32-bit elements; how exact they have to be, the bound alone decides.
A program may use at most 64 MiB of HBM per device.

```python
import math
import jax
import jax.numpy as jnp
from jax import lax

DIM = 256
K = 64
ITERS = 3
PTS_DEV = 2048
NPTS = 32768
ROWDEVS = 16
N_ROWS = 8
N_SUB = 2


def draw_points(key, part):
    key = jax.random.fold_in(key, 1)
    first, second, third = jax.random.split(key, 3)
    base = jnp.clip(jax.random.normal(first, (DIM, NPTS), jnp.float32), -6.0, 6.0)
    feat = jnp.exp(jax.random.uniform(second, (DIM, 1), jnp.float32, math.log(0.6), math.log(1.8)))
    weight = jnp.exp(jax.random.uniform(third, (1, NPTS), jnp.float32, math.log(0.5), math.log(1.5)))
    return base * feat * weight


def bell_draw(key, shape, spread, most, kind=jnp.bfloat16):
    return jnp.clip(spread * jax.random.normal(key, shape, jnp.float32), -most, most).astype(kind)


def setup_inputs(seed: int = 0, part: int = 0) -> dict:
    key_list = jax.random.split(jax.random.key(seed), 4)
    part_splits = jax.random.split(jax.random.fold_in(key_list[3], part), 4)
    points = draw_points(jax.random.fold_in(jax.random.fold_in(key_list[3], part), 71), part)
    start_block = bell_draw(key_list[1], (DIM, K), 1.0, 6.0, jnp.float32)
    median_order = jax.vmap(lambda own: jax.random.permutation(own, PTS_DEV))(jax.random.split(part_splits[2], ROWDEVS)).reshape((ROWDEVS, PTS_DEV)).astype(jnp.int32)
    return dict(points=points, start_block=start_block, median_order=median_order)


HI = lax.Precision.HIGHEST

def orthonormal(wblock):
    gram = jnp.dot(wblock.T, wblock, precision=HI)
    lower = jnp.linalg.cholesky(gram)
    return jax.scipy.linalg.solve_triangular(lower, wblock.T, lower=True).T

def to_children(values, median_order):
    feats = values.shape[0]
    width = PTS_DEV // N_ROWS
    grid = values.reshape(feats, N_ROWS * N_SUB, PTS_DEV)
    sent = jnp.take_along_axis(grid, median_order[None, :, :].astype(jnp.int32), axis=2)
    sent = sent.reshape(feats, N_ROWS, N_SUB, N_ROWS, width)
    return sent.transpose(0, 3, 2, 1, 4).reshape(feats, N_ROWS * N_SUB * PTS_DEV)

def reference(points, start_block, median_order):
    scale = 1.0 / points.shape[1]
    block = start_block
    for step in range(ITERS):
        coords = jnp.dot(block.T, points, precision=HI)
        wblock = lax.dot_general(points, coords, (((1,), (1,)), ((), ())), precision=HI) * scale
        block = orthonormal(wblock)
    coords = jnp.dot(block.T, points, precision=HI)
    return (to_children(points, median_order), to_children(coords, median_order))
```

```python
import functools
import jax
import jax.numpy as jnp
from jax import lax
from jax.experimental import pallas as pl
from jax.experimental.pallas import tpu as pltpu
from jax.sharding import PartitionSpec as P

ITERS = 3


HI = lax.Precision.HIGHEST
MESH = pl.DeviceIdType.MESH
NT = (((1,), (1,)), ((), ()))


def orthonormal(wblock, gram):
    lower = jnp.linalg.cholesky(gram)
    return jax.scipy.linalg.solve_triangular(lower, wblock.T, lower=True).T


def weighted(points, coords, scale):
    return lax.dot_general(points, coords, NT, precision=HI) * scale


def body(points, start_block, median_order):
    total = points.shape[1] * lax.axis_size("rows") * lax.axis_size("sub")
    scale = 1.0 / total
    coords = None

    def project(block):
        return lax.psum(jnp.dot(block.T, points, precision=HI), "cols")

    block = start_block
    for step in range(ITERS):
        coords = project(block)
        partial_value = weighted(points, coords, scale)
        wblock = lax.psum(partial_value, ("rows", "sub"))
        gram = lax.psum(jnp.dot(wblock.T, wblock, precision=HI), "cols")
        block = orthonormal(wblock, gram)
    coords = project(block)
    order = median_order[0]
    sent_points = jnp.take(points, order, axis=1)
    sent_coords = jnp.take(coords, order, axis=1)
    moved_points, moved_coords = (
        lax.all_to_all(sent_points, "rows", split_axis=1, concat_axis=1, tiled=True),
        lax.all_to_all(sent_coords, "rows", split_axis=1, concat_axis=1, tiled=True),
    )
    return (moved_points, moved_coords)


def eliminate(gram, wide):
    size = gram.shape[0]
    done = []
    for base in range(0, size, 8):
        rows = lax.broadcasted_iota(jnp.int32, (gram.shape[0], 1), 0)
        for kk in range(8):
            k = base + kk
            row_g = gram[kk : kk + 1, :]
            inv = 1.0 / row_g[:, k : k + 1]
            col = jnp.where(rows > kk, gram[:, k : k + 1], 0.0)
            row_w = wide[kk : kk + 1, :] * inv
            row_g = row_g * inv
            gram = gram - col * row_g
            wide = wide - col * row_w
        lanes = lax.broadcasted_iota(jnp.int32, (8, size), 1)
        subl = lax.broadcasted_iota(jnp.int32, (8, size), 0)
        diag = jnp.sum(jnp.where(lanes == subl + base, gram[:8], 0.0), axis=1, keepdims=True)
        done.append(wide[:8] * lax.rsqrt(diag))
        gram, wide = gram[8:], wide[8:]
    return jnp.concatenate(done, axis=0)


def kernel(n, scale, pts, sb, order, mp, mc, pieces, moment, pair_in, half, rs_in, whole,
           block, out_buf, in_buf, pair_s, pair_r, rs_s, rs_r, ag_s, ag_r, back_s, back_r,
           ch_s, ch_r, loc):
    me, sub = lax.axis_index("rows"), lax.axis_index("sub")
    other = 1 - sub
    dim, width = pts.shape[0], pts.shape[1] // n
    hd = dim // 2
    sl = hd // n

    barrier = pltpu.get_barrier_semaphore()
    for o in range(1, n):
        pl.semaphore_signal(barrier, inc=1, device_id={"rows": lax.rem(me + o, n)}, device_id_type=MESH)
    pl.semaphore_signal(barrier, inc=1, device_id={"sub": other}, device_id_type=MESH)

    x = pts[...]
    hi = x.astype(jnp.bfloat16)
    rest = x - hi.astype(jnp.float32)
    mid = rest.astype(jnp.bfloat16)
    low = (rest - mid.astype(jnp.float32)).astype(jnp.bfloat16)
    pieces[0:dim, :] = hi
    pieces[dim : 2 * dim, :] = mid
    pieces[2 * dim :, :] = low

    first = lax.dot_general(pieces[...], pieces[0:dim, :], NT, preferred_element_type=jnp.float32)
    mm = lax.dot_general(pieces[dim : 2 * dim, :], pieces[dim : 2 * dim, :], NT,
                         preferred_element_type=jnp.float32)
    cross = first[dim : 2 * dim] + first[2 * dim :]
    moment[...] = first[0:dim] + ((cross + cross.T) + mm)
    pl.semaphore_wait(barrier, n)

    def rows_of(which, start_rows, count):
        return pl.ds(pl.multiple_of(which * start_rows, start_rows), count)

    def remote(src, dst, s, r, **dev):
        return pltpu.make_async_remote_copy(
            src_ref=src, dst_ref=dst, send_sem=s, recv_sem=r, device_id=dev, device_id_type=MESH)

    def off(t):
        return n // 2 + (1 - 2 * (t % 2)) * ((t + 1) // 2)

    def permuted(dest):
        idx = order[:, pl.ds(pl.multiple_of(dest * width, width), width)]
        place = lax.broadcasted_iota(jnp.int32, (pts.shape[1], width), 0)
        hot = jnp.where(place == idx, 1.0, 0.0).astype(jnp.bfloat16)
        got = jnp.dot(pieces[...], hot, preferred_element_type=jnp.float32)
        return got[0:dim] + got[dim : 2 * dim] + got[2 * dim :]

    chunk_sends = []

    def chunk(t):
        dest = lax.rem(me + off(t), n)
        out_buf[t] = permuted(dest)
        c = remote(out_buf.at[t], in_buf.at[me], ch_s.at[t], ch_r.at[me], rows=dest)
        c.start()
        chunk_sends.append(c)

    pair = remote(moment.at[rows_of(other, hd, hd)], pair_in, pair_s, pair_r, sub=other)
    pair.start()
    chunk(0)
    pair.wait()
    half[...] = moment[rows_of(sub, hd, hd), :] + pair_in[...]
    rs = []
    for o in range(1, n):
        q = lax.rem(me + o, n)
        c = remote(half.at[rows_of(q, sl, sl)], rs_in.at[me], rs_s.at[o], rs_r.at[me], rows=q)
        c.start()
        rs.append(c)
    rs_in[me] = half[rows_of(me, sl, sl), :]
    chunk(1)
    chunk(2)
    for o in range(1, n):
        q = lax.rem(me + o, n)
        remote(half.at[rows_of(q, sl, sl)], rs_in.at[q], rs_s.at[o], rs_r.at[q], rows=q).wait_recv()
    mine = pl.ds(pl.multiple_of(sub * hd + me * sl, sl), sl)
    whole[mine, :] = jnp.sum(rs_in[...], axis=0) * scale
    ag = []
    for o in range(1, n):
        q = lax.rem(me + o, n)
        c = remote(whole.at[mine], whole.at[mine], ag_s.at[o], ag_r.at[me], rows=q)
        c.start()
        ag.append(c)
    chunk(3)
    chunk(4)
    for o in range(1, n):
        q = lax.rem(me + o, n)
        theirs = pl.ds(pl.multiple_of(sub * hd + q * sl, sl), sl)
        remote(whole.at[theirs], whole.at[theirs], ag_s.at[o], ag_r.at[q], rows=q).wait_recv()
    own_half = rows_of(sub, hd, hd)
    back = remote(whole.at[own_half], whole.at[own_half], back_s, back_r, sub=other)
    back.start()
    for t in range(5, n - 1):
        chunk(t)
    in_buf[me] = permuted(me)
    back.wait()

    block[...] = sb[...].T

    @pl.loop(0, ITERS)
    def _(step):
        wide = jnp.dot(block[...], whole[...], precision=HI, preferred_element_type=jnp.float32)
        gram = lax.dot_general(wide, wide, NT, precision=HI, preferred_element_type=jnp.float32)
        block[...] = eliminate(gram, wide)

    outs = []
    for t in list(range(n - 1, n)) + list(range(n - 2, -1, -1)):
        src = lax.rem(me + n - off(t), n)
        if t < n - 1:
            remote(out_buf.at[t], in_buf.at[src], ch_s.at[t], ch_r.at[src], rows=src).wait_recv()
        cols = pl.ds(pl.multiple_of(src * width, width), width)
        c = pltpu.make_async_copy(in_buf.at[src], mp.at[:, cols], loc.at[t])
        c.start()
        outs.append(c)
        mc[:, cols] = jnp.dot(block[...], in_buf[src], precision=HI, preferred_element_type=jnp.float32)
    for c in outs:
        c.wait()
    for c in chunk_sends + rs + ag:
        c.wait_send()


def fused(points, start_block, median_order):
    n = lax.axis_size("rows")
    dim, count = points.shape
    k = start_block.shape[1]
    width, hd = count // n, dim // 2
    scale = 1.0 / (count * n * lax.axis_size("sub"))
    f32 = jnp.float32
    vm, dma = pltpu.VMEM, pltpu.SemaphoreType.DMA
    return pl.pallas_call(
        functools.partial(kernel, n, scale),
        out_shape=(jax.ShapeDtypeStruct((dim, count), f32), jax.ShapeDtypeStruct((k, count), f32)),
        in_specs=[pl.BlockSpec(memory_space=vm)] * 3,
        out_specs=(pl.BlockSpec(memory_space=pl.ANY), pl.BlockSpec(memory_space=vm)),
        scratch_shapes=[
            vm((3 * dim, count), jnp.bfloat16),
            vm((dim, dim), f32),
            vm((hd, dim), f32),
            vm((hd, dim), f32),
            vm((n, hd // n, dim), f32),
            vm((dim, dim), f32),
            vm((k, dim), f32),
            vm((n, dim, width), f32),
            vm((n, dim, width), f32),
            dma, dma, dma((n,)), dma((n,)), dma((n,)), dma((n,)), dma, dma,
            dma((n,)), dma((n,)), dma((n,)),
        ],
        compiler_params=pltpu.CompilerParams(
            collective_id=0, has_side_effects=True, vmem_limit_bytes=48 * 1024 * 1024),
    )(points, start_block, median_order)


def solution(mesh):
    in_specs = (
        P("cols", ("groups", "rows", "sub")),
        P("cols", None),
        P(("groups", "rows", "sub"), None),
    )
    out_specs = (P("cols", ("groups", "rows", "sub")), P(None, ("groups", "rows", "sub")))
    whole_features = mesh.shape["cols"] == 1 and mesh.shape["sub"] == 2
    return jax.shard_map(fused if whole_features else body, mesh=mesh, in_specs=in_specs,
                         out_specs=out_specs, check_vma=False)
```

```python
import functools
import jax
import jax.numpy as jnp
from jax import lax
from jax.experimental import pallas as pl
from jax.experimental.pallas import tpu as pltpu
from jax.sharding import PartitionSpec as P

ITERS = 3


HI = lax.Precision.HIGHEST
EARLY, MIDDLE, LATE = 1, 1, 2
ORDERS = ((4, 2, 6, 3, 5, 1, 7), (2, 4, 3, 6, 1, 5, 7))
MESH = pl.DeviceIdType.MESH
NT = (((1,), (1,)), ((), ()))


def orthonormal(wblock, gram):
    lower = jnp.linalg.cholesky(gram)
    return jax.scipy.linalg.solve_triangular(lower, wblock.T, lower=True).T


def weighted(points, coords, scale):
    return lax.dot_general(points, coords, NT, precision=HI) * scale


def body(points, start_block, median_order):
    total = points.shape[1] * lax.axis_size("rows") * lax.axis_size("sub")
    scale = 1.0 / total
    coords = None

    def project(block):
        return lax.psum(jnp.dot(block.T, points, precision=HI), "cols")

    block = start_block
    for step in range(ITERS):
        coords = project(block)
        partial_value = weighted(points, coords, scale)
        wblock = lax.psum(partial_value, ("rows", "sub"))
        gram = lax.psum(jnp.dot(wblock.T, wblock, precision=HI), "cols")
        block = orthonormal(wblock, gram)
    coords = project(block)
    order = median_order[0]
    sent_points = jnp.take(points, order, axis=1)
    sent_coords = jnp.take(coords, order, axis=1)
    moved_points, moved_coords = (
        lax.all_to_all(sent_points, "rows", split_axis=1, concat_axis=1, tiled=True),
        lax.all_to_all(sent_coords, "rows", split_axis=1, concat_axis=1, tiled=True),
    )
    return (moved_points, moved_coords)


def eliminate(gram, wide):
    size = gram.shape[0]
    done = []
    for base in range(0, size, 8):
        rows = lax.broadcasted_iota(jnp.int32, (gram.shape[0], 1), 0)
        for kk in range(8):
            k = base + kk
            row_g = gram[kk : kk + 1, :]
            inv = 1.0 / row_g[:, k : k + 1]
            col = jnp.where(rows > kk, gram[:, k : k + 1], 0.0)
            row_w = wide[kk : kk + 1, :] * inv
            row_g = row_g * inv
            gram = gram - col * row_g
            wide = wide - col * row_w
        lanes = lax.broadcasted_iota(jnp.int32, (8, size), 1)
        subl = lax.broadcasted_iota(jnp.int32, (8, size), 0)
        diag = jnp.sum(jnp.where(lanes == subl + base, gram[:8], 0.0), axis=1, keepdims=True)
        done.append(wide[:8] * lax.rsqrt(diag))
        gram, wide = gram[8:], wide[8:]
    return jnp.concatenate(done, axis=0)


def kernel(n, scale, pts_hbm, sb, order, mp, mc, pieces, moment, pair_in, half, rs_in, whole,
           block, out_buf, in_buf, pair_s, pair_r, rs_s, rs_r, ag_s, ag_r, back_s, back_r,
           ch_s, ch_r, loc, pts, ld):
    me, sub = lax.axis_index("rows"), lax.axis_index("sub")
    other = 1 - sub
    dim, width = pts.shape[0], pts.shape[1] // n
    hd = dim // 2
    sl = hd // n

    loads = []
    for i in range(n):
        c = pltpu.make_async_copy(pts_hbm.at[:, i * width : (i + 1) * width],
                                  pts.at[:, i * width : (i + 1) * width], ld.at[i])
        c.start()
        loads.append(c)

    barrier = pltpu.get_barrier_semaphore()
    for o in range(1, n):
        pl.semaphore_signal(barrier, inc=1, device_id={"rows": lax.rem(me + o, n)}, device_id_type=MESH)
    pl.semaphore_signal(barrier, inc=1, device_id={"sub": other}, device_id_type=MESH)

    for i in range(n):
        part = pl.ds(i * width, width)
        loads[i].wait()
        x = pts[:, part]
        hi = x.astype(jnp.bfloat16)
        rest = x - hi.astype(jnp.float32)
        mid = rest.astype(jnp.bfloat16)
        pieces[0:dim, part] = hi
        pieces[dim : 2 * dim, part] = mid
        pieces[2 * dim :, part] = (rest - mid.astype(jnp.float32)).astype(jnp.bfloat16)
    pl.semaphore_wait(barrier, n)

    def rows_of(which, start_rows, count):
        return pl.ds(pl.multiple_of(which * start_rows, start_rows), count)

    def remote(src, dst, s, r, **dev):
        return pltpu.make_async_remote_copy(
            src_ref=src, dst_ref=dst, send_sem=s, recv_sem=r, device_id=dev, device_id_type=MESH)

    def peer(t):
        first_c, second_c = ORDERS[0][t], ORDERS[1][t]
        c = first_c + sub * (second_c - first_c)
        dest, bit = me, 1
        while bit < n:
            dest = dest + lax.rem(c // bit, 2) * (1 - 2 * lax.rem(me // bit, 2)) * bit
            bit *= 2
        return dest

    def permuted(dest):
        idx = order[:, pl.ds(pl.multiple_of(dest * width, width), width)]
        place = lax.broadcasted_iota(jnp.int32, (pts.shape[1], width), 0)
        hot = jnp.where(place == idx, 1.0, 0.0).astype(jnp.bfloat16)
        got = jnp.dot(pieces[...], hot, preferred_element_type=jnp.float32)
        return got[0:dim] + got[dim : 2 * dim] + got[2 * dim :]

    chunk_sends = []

    def permute(t):
        out_buf[t] = permuted(peer(t))

    def send(t):
        dest = peer(t)
        c = remote(out_buf.at[t], in_buf.at[me], ch_s.at[t], ch_r.at[me], rows=dest)
        c.start()
        chunk_sends.append(c)

    for t in range(EARLY):
        permute(t)
        send(t)
    first = lax.dot_general(pieces[...], pieces[0:dim, :], NT, preferred_element_type=jnp.float32)
    mm = lax.dot_general(pieces[dim : 2 * dim, :], pieces[dim : 2 * dim, :], NT,
                         preferred_element_type=jnp.float32)
    cross = first[dim : 2 * dim] + first[2 * dim :]
    moment[...] = first[0:dim] + ((cross + cross.T) + mm)
    pair = remote(moment.at[rows_of(other, hd, hd)], pair_in, pair_s, pair_r, sub=other)
    pair.start()
    permute(EARLY)
    pair.wait()
    half[...] = moment[rows_of(sub, hd, hd), :] + pair_in[...]
    rs = []
    for o in range(1, n):
        q = lax.rem(me + o, n)
        c = remote(half.at[rows_of(q, sl, sl)], rs_in.at[me], rs_s.at[o], rs_r.at[me], rows=q)
        c.start()
        rs.append(c)
    rs_in[me] = half[rows_of(me, sl, sl), :]
    for t in range(EARLY, MIDDLE):
        send(t)
    for t in range(EARLY + 1, n - 1):
        permute(t)
    for o in range(1, n):
        q = lax.rem(me + o, n)
        remote(half.at[rows_of(q, sl, sl)], rs_in.at[q], rs_s.at[o], rs_r.at[q], rows=q).wait_recv()
    mine = pl.ds(pl.multiple_of(sub * hd + me * sl, sl), sl)
    whole[mine, :] = jnp.sum(rs_in[...], axis=0) * scale
    ag = []
    for o in range(1, n):
        q = lax.rem(me + o, n)
        c = remote(whole.at[mine], whole.at[mine], ag_s.at[o], ag_r.at[me], rows=q)
        c.start()
        ag.append(c)
    for t in range(MIDDLE, LATE):
        send(t)
    in_buf[me] = permuted(me)
    block[...] = sb[...].T
    for o in range(1, n):
        q = lax.rem(me + o, n)
        theirs = pl.ds(pl.multiple_of(sub * hd + q * sl, sl), sl)
        remote(whole.at[theirs], whole.at[theirs], ag_s.at[o], ag_r.at[q], rows=q).wait_recv()
    own_half = rows_of(sub, hd, hd)
    back = remote(whole.at[own_half], whole.at[own_half], back_s, back_r, sub=other)
    back.start()
    for t in range(LATE, n - 1):
        send(t)
    back.wait()

    @pl.loop(0, ITERS)
    def _(step):
        wide = jnp.dot(block[...], whole[...], precision=HI, preferred_element_type=jnp.float32)
        gram = lax.dot_general(wide, wide, NT, precision=HI, preferred_element_type=jnp.float32)
        block[...] = eliminate(gram, wide)

    outs = []
    for t in [n - 1] + list(range(n - 1)):
        src = me if t == n - 1 else peer(t)
        if t < n - 1:
            remote(out_buf.at[t], in_buf.at[src], ch_s.at[t], ch_r.at[src], rows=src).wait_recv()
        cols = pl.ds(pl.multiple_of(src * width, width), width)
        c = pltpu.make_async_copy(in_buf.at[src], mp.at[:, cols], loc.at[t])
        c.start()
        outs.append(c)
        mc[:, cols] = jnp.dot(block[...], in_buf[src], precision=HI, preferred_element_type=jnp.float32)
    for c in outs:
        c.wait()
    for c in chunk_sends + rs + ag:
        c.wait_send()


def fused(points, start_block, median_order):
    n = lax.axis_size("rows")
    dim, count = points.shape
    k = start_block.shape[1]
    width, hd = count // n, dim // 2
    scale = 1.0 / (count * n * lax.axis_size("sub"))
    f32 = jnp.float32
    vm, dma = pltpu.VMEM, pltpu.SemaphoreType.DMA
    return pl.pallas_call(
        functools.partial(kernel, n, scale),
        out_shape=(jax.ShapeDtypeStruct((dim, count), f32), jax.ShapeDtypeStruct((k, count), f32)),
        in_specs=[pl.BlockSpec(memory_space=pl.ANY)] + [pl.BlockSpec(memory_space=vm)] * 2,
        out_specs=(pl.BlockSpec(memory_space=pl.ANY), pl.BlockSpec(memory_space=vm)),
        scratch_shapes=[
            vm((3 * dim, count), jnp.bfloat16),
            vm((dim, dim), f32),
            vm((hd, dim), f32),
            vm((hd, dim), f32),
            vm((n, hd // n, dim), f32),
            vm((dim, dim), f32),
            vm((k, dim), f32),
            vm((n, dim, width), f32),
            vm((n, dim, width), f32),
            dma, dma, dma((n,)), dma((n,)), dma((n,)), dma((n,)), dma, dma,
            dma((n,)), dma((n,)), dma((n,)),
            vm((dim, count), f32), dma((n,)),
        ],
        compiler_params=pltpu.CompilerParams(
            collective_id=0, has_side_effects=True, vmem_limit_bytes=48 * 1024 * 1024),
    )(points, start_block, median_order)


def solution(mesh):
    in_specs = (
        P("cols", ("groups", "rows", "sub")),
        P("cols", None),
        P(("groups", "rows", "sub"), None),
    )
    out_specs = (P("cols", ("groups", "rows", "sub")), P(None, ("groups", "rows", "sub")))
    peers = len(ORDERS[0])
    whole_features = mesh.shape["cols"] == 1 and mesh.shape["sub"] == 2 and mesh.shape["rows"] == peers + 1
    return jax.shard_map(fused if whole_features else body, mesh=mesh, in_specs=in_specs,
                         out_specs=out_specs, check_vma=False)
```

```python
import functools
import jax
import jax.numpy as jnp
from jax import lax
from jax.experimental import pallas as pl
from jax.experimental.pallas import tpu as pltpu
from jax.sharding import PartitionSpec as P

ITERS = 3


HI = lax.Precision.HIGHEST
EARLY, MIDDLE, LATE = 1, 1, 3
ORDERS = ((4, 2, 6, 3, 5, 1, 7), (2, 4, 3, 6, 1, 5, 7))
MESH = pl.DeviceIdType.MESH
NT = (((1,), (1,)), ((), ()))


def orthonormal(wblock, gram):
    lower = jnp.linalg.cholesky(gram)
    return jax.scipy.linalg.solve_triangular(lower, wblock.T, lower=True).T


def weighted(points, coords, scale):
    return lax.dot_general(points, coords, NT, precision=HI) * scale


def body(points, start_block, median_order):
    total = points.shape[1] * lax.axis_size("rows") * lax.axis_size("sub")
    scale = 1.0 / total
    coords = None

    def project(block):
        return lax.psum(jnp.dot(block.T, points, precision=HI), "cols")

    block = start_block
    for step in range(ITERS):
        coords = project(block)
        partial_value = weighted(points, coords, scale)
        wblock = lax.psum(partial_value, ("rows", "sub"))
        gram = lax.psum(jnp.dot(wblock.T, wblock, precision=HI), "cols")
        block = orthonormal(wblock, gram)
    coords = project(block)
    order = median_order[0]
    sent_points = jnp.take(points, order, axis=1)
    sent_coords = jnp.take(coords, order, axis=1)
    moved_points, moved_coords = (
        lax.all_to_all(sent_points, "rows", split_axis=1, concat_axis=1, tiled=True),
        lax.all_to_all(sent_coords, "rows", split_axis=1, concat_axis=1, tiled=True),
    )
    return (moved_points, moved_coords)


def eliminate(gram, wide):
    size = gram.shape[0]
    done = []
    for base in range(0, size, 8):
        rows = lax.broadcasted_iota(jnp.int32, (gram.shape[0], 1), 0)
        for kk in range(8):
            k = base + kk
            row_g = gram[kk : kk + 1, :]
            inv = 1.0 / row_g[:, k : k + 1]
            col = jnp.where(rows > kk, gram[:, k : k + 1], 0.0)
            row_w = wide[kk : kk + 1, :] * inv
            row_g = row_g * inv
            gram = gram - col * row_g
            wide = wide - col * row_w
        lanes = lax.broadcasted_iota(jnp.int32, (8, size), 1)
        subl = lax.broadcasted_iota(jnp.int32, (8, size), 0)
        diag = jnp.sum(jnp.where(lanes == subl + base, gram[:8], 0.0), axis=1, keepdims=True)
        done.append(wide[:8] * lax.rsqrt(diag))
        gram, wide = gram[8:], wide[8:]
    return jnp.concatenate(done, axis=0)


def kernel(n, scale, pts_hbm, sb, order, mp, mc, pieces, moment, pair_in, half, rs_in, whole,
           block, out_buf, in_buf, pair_s, pair_r, rs_s, rs_r, ag_s, ag_r, back_s, back_r,
           ch_s, ch_r, loc, pts, ld):
    me, sub = lax.axis_index("rows"), lax.axis_index("sub")
    other = 1 - sub
    dim, width = pts.shape[0], pts.shape[1] // n
    hd = dim // 2
    sl = hd // n

    loads = []
    for i in range(n):
        c = pltpu.make_async_copy(pts_hbm.at[:, i * width : (i + 1) * width],
                                  pts.at[:, i * width : (i + 1) * width], ld.at[i])
        c.start()
        loads.append(c)

    barrier = pltpu.get_barrier_semaphore()
    for o in range(1, n):
        pl.semaphore_signal(barrier, inc=1, device_id={"rows": lax.rem(me + o, n)}, device_id_type=MESH)
    pl.semaphore_signal(barrier, inc=1, device_id={"sub": other}, device_id_type=MESH)

    for i in range(n):
        part = pl.ds(i * width, width)
        loads[i].wait()
        x = pts[:, part]
        hi = x.astype(jnp.bfloat16)
        rest = x - hi.astype(jnp.float32)
        mid = rest.astype(jnp.bfloat16)
        pieces[0:dim, part] = hi
        pieces[dim : 2 * dim, part] = mid
        pieces[2 * dim :, part] = (rest - mid.astype(jnp.float32)).astype(jnp.bfloat16)
    pl.semaphore_wait(barrier, n)

    def rows_of(which, start_rows, count):
        return pl.ds(pl.multiple_of(which * start_rows, start_rows), count)

    def remote(src, dst, s, r, **dev):
        return pltpu.make_async_remote_copy(
            src_ref=src, dst_ref=dst, send_sem=s, recv_sem=r, device_id=dev, device_id_type=MESH)

    def peer(t):
        first_c, second_c = ORDERS[0][t], ORDERS[1][t]
        c = first_c + sub * (second_c - first_c)
        dest, bit = me, 1
        while bit < n:
            dest = dest + lax.rem(c // bit, 2) * (1 - 2 * lax.rem(me // bit, 2)) * bit
            bit *= 2
        return dest

    def permuted(dest):
        idx = order[:, pl.ds(pl.multiple_of(dest * width, width), width)]
        place = lax.broadcasted_iota(jnp.int32, (pts.shape[1], width), 0)
        hot = jnp.where(place == idx, 1.0, 0.0).astype(jnp.bfloat16)
        got = jnp.dot(pieces[...], hot, preferred_element_type=jnp.float32)
        return got[0:dim] + got[dim : 2 * dim] + got[2 * dim :]

    chunk_sends = []

    def permute(t):
        out_buf[t] = permuted(peer(t))

    def send(t):
        dest = peer(t)
        c = remote(out_buf.at[t], in_buf.at[me], ch_s.at[t], ch_r.at[me], rows=dest)
        c.start()
        chunk_sends.append(c)

    for t in range(EARLY):
        permute(t)
        send(t)
    first = lax.dot_general(pieces[...], pieces[0:dim, :], NT, preferred_element_type=jnp.float32)
    mm = lax.dot_general(pieces[dim : 2 * dim, :], pieces[dim : 2 * dim, :], NT,
                         preferred_element_type=jnp.float32)
    cross = first[dim : 2 * dim] + first[2 * dim :]
    moment[...] = first[0:dim] + ((cross + cross.T) + mm)
    pair = remote(moment.at[rows_of(other, hd, hd)], pair_in, pair_s, pair_r, sub=other)
    pair.start()
    permute(EARLY)
    pair.wait()
    half[...] = moment[rows_of(sub, hd, hd), :] + pair_in[...]
    rs = []
    for o in range(1, n):
        q = lax.rem(me + o, n)
        c = remote(half.at[rows_of(q, sl, sl)], rs_in.at[me], rs_s.at[o], rs_r.at[me], rows=q)
        c.start()
        rs.append(c)
    rs_in[me] = half[rows_of(me, sl, sl), :]
    for t in range(EARLY, MIDDLE):
        send(t)
    for t in range(EARLY + 1, n - 1):
        permute(t)
    for o in range(1, n):
        q = lax.rem(me + o, n)
        remote(half.at[rows_of(q, sl, sl)], rs_in.at[q], rs_s.at[o], rs_r.at[q], rows=q).wait_recv()
    mine = pl.ds(pl.multiple_of(sub * hd + me * sl, sl), sl)
    whole[mine, :] = jnp.sum(rs_in[...], axis=0) * scale
    ag = []
    for o in range(1, n):
        q = lax.rem(me + o, n)
        c = remote(whole.at[mine], whole.at[mine], ag_s.at[o], ag_r.at[me], rows=q)
        c.start()
        ag.append(c)
    for t in range(MIDDLE, LATE):
        send(t)
    in_buf[me] = permuted(me)
    block[...] = sb[...].T
    for o in range(1, n):
        q = lax.rem(me + o, n)
        theirs = pl.ds(pl.multiple_of(sub * hd + q * sl, sl), sl)
        remote(whole.at[theirs], whole.at[theirs], ag_s.at[o], ag_r.at[q], rows=q).wait_recv()
    own_half = rows_of(sub, hd, hd)
    back = remote(whole.at[own_half], whole.at[own_half], back_s, back_r, sub=other)
    back.start()
    for t in range(LATE, n - 1):
        send(t)
    back.wait()

    @pl.loop(0, ITERS)
    def _(step):
        wide = jnp.dot(block[...], whole[...], precision=HI, preferred_element_type=jnp.float32)
        gram = lax.dot_general(wide, wide, NT, precision=HI, preferred_element_type=jnp.float32)
        block[...] = eliminate(gram, wide)

    outs = []
    for t in [n - 1] + list(range(n - 1)):
        src = me if t == n - 1 else peer(t)
        if t < n - 1:
            remote(out_buf.at[t], in_buf.at[src], ch_s.at[t], ch_r.at[src], rows=src).wait_recv()
        cols = pl.ds(pl.multiple_of(src * width, width), width)
        c = pltpu.make_async_copy(in_buf.at[src], mp.at[:, cols], loc.at[t])
        c.start()
        outs.append(c)
        mc[:, cols] = jnp.dot(block[...], in_buf[src], precision=HI, preferred_element_type=jnp.float32)
    for c in outs:
        c.wait()
    for c in chunk_sends + rs + ag:
        c.wait_send()


def fused(points, start_block, median_order):
    n = lax.axis_size("rows")
    dim, count = points.shape
    k = start_block.shape[1]
    width, hd = count // n, dim // 2
    scale = 1.0 / (count * n * lax.axis_size("sub"))
    f32 = jnp.float32
    vm, dma = pltpu.VMEM, pltpu.SemaphoreType.DMA
    return pl.pallas_call(
        functools.partial(kernel, n, scale),
        out_shape=(jax.ShapeDtypeStruct((dim, count), f32), jax.ShapeDtypeStruct((k, count), f32)),
        in_specs=[pl.BlockSpec(memory_space=pl.ANY)] + [pl.BlockSpec(memory_space=vm)] * 2,
        out_specs=(pl.BlockSpec(memory_space=pl.ANY), pl.BlockSpec(memory_space=vm)),
        scratch_shapes=[
            vm((3 * dim, count), jnp.bfloat16),
            vm((dim, dim), f32),
            vm((hd, dim), f32),
            vm((hd, dim), f32),
            vm((n, hd // n, dim), f32),
            vm((dim, dim), f32),
            vm((k, dim), f32),
            vm((n, dim, width), f32),
            vm((n, dim, width), f32),
            dma, dma, dma((n,)), dma((n,)), dma((n,)), dma((n,)), dma, dma,
            dma((n,)), dma((n,)), dma((n,)),
            vm((dim, count), f32), dma((n,)),
        ],
        compiler_params=pltpu.CompilerParams(
            collective_id=0, has_side_effects=True, vmem_limit_bytes=48 * 1024 * 1024),
    )(points, start_block, median_order)


def solution(mesh):
    in_specs = (
        P("cols", ("groups", "rows", "sub")),
        P("cols", None),
        P(("groups", "rows", "sub"), None),
    )
    out_specs = (P("cols", ("groups", "rows", "sub")), P(None, ("groups", "rows", "sub")))
    peers = len(ORDERS[0])
    whole_features = mesh.shape["cols"] == 1 and mesh.shape["sub"] == 2 and mesh.shape["rows"] == peers + 1
    return jax.shard_map(fused if whole_features else body, mesh=mesh, in_specs=in_specs,
                         out_specs=out_specs, check_vma=False)
```
